32 devices in a mesh: lon: 8 (over y, x, core), lat: 4 (over z).
Axes of the slice: x: 2, y: 2, z: 4, core: 2. Of those that a mesh axis runs over, the one named last changes fastest.
Arguments:
- height: float32 [768, 7200], P('lat', 'lon'), may hold values from 0.4 to 1.6
- east_wind: float32 [768, 7200], P('lat', 'lon'), may hold values from -1.5 to 1.5
- north_wind: float32 [768, 7200], P('lat', 'lon'), may hold values from -1.5 to 1.5
- cutoffs: int32 [512], replicated, may hold values from 1 to 64
Outputs:
- height_final: float32 [768, 7200], P('lat', 'lon')
- east_final: float32 [768, 7200], P('lat', 'lon')
- north_final: float32 [768, 7200], P('lat', 'lon')
The draws below stay inside these ranges and needn't reach their ends.
All inputs are finite; a program needn't handle non-finite values.
Results may differ from the reference program's by a relative error of at most 0.0002.
Values sent between devices are 32-bit elements; how exact they have to be, the bound alone decides.
A program may use at most 128 MiB of HBM per device.

```python
import math
import jax
import jax.numpy as jnp

NLON = 7200
LAT_ROWS = 3600
KMAX = 64
STEPS = 2
ROWS = 768
FROWS = 512


def cutoff_rows(key):
    rows = jnp.arange(FROWS, dtype=jnp.int32)
    jitter = jax.random.randint(jax.random.fold_in(key, 11), (FROWS,), 0, 3) * (rows > 0).astype(jnp.int32)
    return jnp.minimum(KMAX, 1 + rows * KMAX // FROWS + jitter).astype(jnp.int32)


def draw_cutoffs(key, part):
    return cutoff_rows(key)


def wave_field(key, salt, middle, rough, wave):
    cutoff = cutoff_rows(key)
    rows = jnp.arange(ROWS, dtype=jnp.int32)
    polar = rows < FROWS
    polar_share = polar.astype(jnp.float32)
    ceiling = jnp.where(polar, cutoff[jnp.minimum(rows, FROWS - 1)], KMAX)
    keys = jax.random.split(jax.random.fold_in(key, salt), 10)
    modes = jax.random.randint(keys[0], (ROWS, 4), 1, ceiling[:, None] + 1)
    offsets = jax.random.randint(keys[1], (ROWS, 4), 0, NLON)
    upper = jnp.minimum(2 * ceiling + 2, NLON // 2)
    extra_modes = jax.random.randint(keys[6], (ROWS, 2), ceiling[:, None] + 1, upper[:, None])
    extra_offsets = jax.random.randint(keys[7], (ROWS, 2), 0, NLON)
    columns = jnp.arange(NLON, dtype=jnp.int32)
    amounts = jax.random.uniform(keys[3], (ROWS, 4), minval=-wave, maxval=wave)
    noise = jax.random.uniform(keys[5], (ROWS, NLON), minval=-rough, maxval=rough)
    extra_amounts = jax.random.uniform(keys[9], (ROWS, 2), minval=-0.5 * rough, maxval=0.5 * rough)
    total = middle + noise * (1.0 - polar_share)[:, None]
    for term in range(2):
        turn = extra_modes[:, term:term + 1] * (columns[None, :] + extra_offsets[:, term:term + 1]) % NLON
        total = total + polar_share[:, None] * extra_amounts[:, term:term + 1] * jnp.cos(turn.astype(jnp.float32) * (2.0 * math.pi / NLON))
    for term in range(4):
        turn = modes[:, term:term + 1] * (columns[None, :] + offsets[:, term:term + 1]) % NLON
        total = total + amounts[:, term:term + 1] * jnp.cos(turn.astype(jnp.float32) * (2.0 * math.pi / NLON))
    return total.astype(jnp.float32)


def draw_height(key, part):
    return wave_field(key, 21, 1.0, 0.2, 0.1)


def draw_east_wind(key, part):
    return wave_field(key, 22, 0.0, 0.3, 0.3)


def draw_north_wind(key, part):
    return wave_field(key, 23, 0.0, 0.3, 0.3)


def setup_inputs(seed: int = 0) -> dict:
    streams_of = jax.random.split(jax.random.key(seed), 5)
    height = draw_height(jax.random.fold_in(streams_of[4], 71), 0)
    east_wind = draw_east_wind(jax.random.fold_in(streams_of[4], 71), 0)
    north_wind = draw_north_wind(jax.random.fold_in(streams_of[4], 71), 0)
    cutoffs = draw_cutoffs(jax.random.fold_in(streams_of[4], 71), 0)
    return {"height": height, "east_wind": east_wind, "north_wind": north_wind, "cutoffs": cutoffs}


COURANT = 0.1
OMEGA_RATE = 1.5


def zonal_diff(field, lon_step):
    return (jnp.roll(field, -1, axis=1) - jnp.roll(field, 1, axis=1)) * (0.5 / lon_step)


def north_diff(field, lat_step):
    return (field[:-2] - field[2:]) * (0.5 / lat_step)


def extend_rows(field, flip):
    mirror = flip * jnp.roll(field[0:1], NLON // 2, axis=1)
    return jnp.concatenate([mirror, field, field[-1:]], axis=0)


def tendency(state, coslat, sinlat, cos_tall, lon_step, lat_step):
    height, east, north = state
    height_tall = extend_rows(height, 1.0)
    east_tall = extend_rows(east, -1.0)
    north_tall = extend_rows(north, -1.0)
    inv_cos = 1.0 / coslat
    turning = 2.0 * OMEGA_RATE * sinlat + east * sinlat * inv_cos
    rate_height = -(zonal_diff(height * east, lon_step) + north_diff(height_tall * north_tall * cos_tall, lat_step)) * inv_cos
    rate_east = -east * zonal_diff(east, lon_step) * inv_cos - north * north_diff(east_tall, lat_step) + turning * north - zonal_diff(height, lon_step) * inv_cos
    rate_north = -east * zonal_diff(north, lon_step) * inv_cos - north * north_diff(north_tall, lat_step) - turning * east - north_diff(height_tall, lat_step)
    return (rate_height, rate_east, rate_north)


def polar_filter(field, cutoffs):
    top = field[:FROWS]
    spectrum = jnp.fft.rfft(top, axis=1)
    waves = jnp.arange(NLON // 2 + 1, dtype=jnp.int32)
    keep = waves[None, :] <= cutoffs[:, None]
    low = jnp.fft.irfft(jnp.where(keep, spectrum, 0.0), n=NLON, axis=1).astype(jnp.float32)
    return jnp.concatenate([low, field[FROWS:]], axis=0)


def reference(height, east_wind, north_wind, cutoffs):
    lat_step = math.pi / LAT_ROWS
    lon_step = 2.0 * math.pi / NLON
    time_step = COURANT * lat_step
    index = jnp.arange(-1, ROWS + 1).astype(jnp.float32)
    cos_all = jnp.abs(jnp.sin((index + 0.5) * lat_step))
    sin_all = jnp.cos((index + 0.5) * lat_step)
    coslat = cos_all[1:-1][:, None]
    sinlat = sin_all[1:-1][:, None]
    cos_tall = cos_all[:, None]
    state = (height, east_wind, north_wind)
    for step_index in range(STEPS):
        rates = tendency(state, coslat, sinlat, cos_tall, lon_step, lat_step)
        middle = tuple(field + (0.5 * time_step) * rate for field, rate in zip(state, rates))
        rates = tendency(middle, coslat, sinlat, cos_tall, lon_step, lat_step)
        state = tuple(polar_filter(field + time_step * rate, cutoffs) for field, rate in zip(state, rates))
    return (state[0], state[1], state[2])
```

```python
import functools
import math

import jax
import jax.numpy as jnp
import numpy as np
from jax import lax
from jax.experimental import pallas as pl
from jax.experimental.pallas import tpu as pltpu
from jax.sharding import PartitionSpec as P

NLON = 7200
LAT_ROWS = 3600
KMAX = 64
STEPS = 2
COURANT = 0.1
OMEGA_RATE = 1.5

LAT_STEP = math.pi / LAT_ROWS
LON_STEP = 2.0 * math.pi / NLON
TIME_STEP = COURANT * LAT_STEP
COEFFS = 2 * KMAX + 1
TOP = 16
HALO = 4
LANES = 128
MESH = pl.DeviceIdType.MESH


def up_to(value, multiple):
    return -(-value // multiple) * multiple


class Plan:
    def __init__(self, lons, lats, rows, width, filtered):
        self.lons, self.lats, self.rows, self.width = lons, lats, rows, width
        self.filtered = filtered
        self.lanes = up_to(width + 2 * HALO, LANES)
        self.tall = rows + 2 * TOP
        self.part = rows + TOP
        self.cols = up_to(3 * self.part, LANES)
        self.share = up_to(COEFFS, lons) // lons
        self.pad = up_to(self.share, 8)
        self.waves = lons * self.pad


def wave_tables(plan):
    index = np.arange(plan.lons)[:, None] * plan.share + np.arange(plan.pad)[None, :]
    real = (np.arange(plan.pad)[None, :] < plan.share) & (index < COEFFS)
    index = np.where(real, index, 0).reshape(-1)
    wave = np.where(index <= KMAX, index, index - KMAX)
    lane = np.arange(plan.lanes)
    local = np.where(lane < plan.lanes - HALO, lane, lane - plan.lanes)
    column = np.arange(plan.lons)[:, None] * plan.width + local[None, :]
    turn = (wave[None, :, None] * column[:, None, :]) % NLON * (2.0 * math.pi / NLON)
    table = np.where((index <= KMAX)[None, :, None], np.cos(turn), np.sin(turn))
    table = np.where(real.reshape(-1)[None, :, None], table, 0.0).astype(np.float32)
    high = table.astype(jnp.bfloat16)
    low = (table - high.astype(np.float32)).astype(jnp.bfloat16)
    return np.stack([high, low], axis=1)


def row_tables(plan):
    row = np.arange(plan.lats)[:, None] * plan.rows + np.arange(plan.tall)[None, :] - TOP
    angle = (row + 0.5) * LAT_STEP
    cos = np.abs(np.sin(angle))
    north = np.abs(np.sin(angle - LAT_STEP))
    south = np.abs(np.sin(angle + LAT_STEP))
    signed = np.where(row < 0, -1.0, 1.0) / cos
    sin = np.cos(angle)
    half = 0.5 / LAT_STEP
    out = np.stack(
        [0.5 / LON_STEP * signed, half * north / cos, half * south / cos, 2.0 * OMEGA_RATE * sin, sin * signed],
        axis=1,
    )
    return np.broadcast_to(out[..., None], out.shape + (LANES,)).astype(np.float32)


def stage(plan, geo, source, base, target, factor):
    spread = plan.lanes // LANES
    half = 0.5 / LAT_STEP

    @pl.loop(1, plan.tall // 8 - 1)
    def _(tile):
        start = pl.multiple_of(tile * 8, 8)
        here = pl.ds(start, 8)
        around = pl.ds(start - 8, 24)
        a, gn, gs, m3, q = (
            jnp.concatenate([geo[g, here, :]] * spread, axis=1) for g in range(5)
        )
        tiles = [source[f, around, :] for f in range(3)]
        h, u, v = (tile[8:16] for tile in tiles)
        hn, un, vn = (tile[7:15] for tile in tiles)
        hs, us, vs = (tile[9:17] for tile in tiles)

        def zonal(value):
            return pltpu.roll(value, plan.lanes - 1, 1) - pltpu.roll(value, 1, 1)

        ua = u * a
        vb = v * half
        m = m3 + u * q
        fh = -(zonal(h * u) * a) - (hn * vn * gn - hs * vs * gs)
        fu = m * v - ua * zonal(u) - vb * (un - us) - zonal(h) * a
        fv = -(m * u) - ua * zonal(v) - vb * (vn - vs) - half * (hn - hs)
        target[0, here, :] = base[0, here, :] + factor * fh
        target[1, here, :] = base[1, here, :] + factor * fu
        target[2, here, :] = base[2, here, :] + factor * fv


def split(value):
    high = value.astype(jnp.bfloat16)
    return high, (value - high.astype(jnp.float32)).astype(jnp.bfloat16)


def kernel(
    plan, h_in, u_in, v_in, cut_ref, waves_hbm, rows_hbm, h_out, u_out, v_out,
    state, middle, strips, north_strips, got_strips, lines, got_lines,
    waves, geo, work, parts, got_parts, whole, coeffs,
    local_sem, strip_send, strip_recv, line_send, line_recv,
    scatter_send, scatter_recv, gather_send, gather_recv,
):
    lon = lax.axis_index("lon")
    lat = lax.axis_index("lat")
    lons, lats, rows, width, lanes = plan.lons, plan.lats, plan.rows, plan.width, plan.lanes
    tall, part, half = plan.tall, plan.part, plan.lons // 2
    last = lats - 1
    end = TOP + rows
    edge = lanes - LANES
    off = width - edge

    get_waves = pltpu.make_async_copy(waves_hbm.at[lon], waves, local_sem.at[0])
    get_rows = pltpu.make_async_copy(rows_hbm.at[lat], geo, local_sem.at[1])
    get_waves.start()
    get_rows.start()

    def around(by):
        return lax.rem(lon + by + lons, lons)

    barrier = pltpu.get_barrier_semaphore()
    for by in range(1, lons):
        pl.semaphore_signal(barrier, inc=1, device_id={"lon": around(by), "lat": lat}, device_id_type=MESH)

    @pl.when(lat > 0)
    def _():
        for by in (-1, 0, 1):
            pl.semaphore_signal(barrier, inc=1, device_id={"lon": around(by), "lat": lat - 1}, device_id_type=MESH)

    @pl.when(lat < last)
    def _():
        for by in (-1, 0, 1):
            pl.semaphore_signal(barrier, inc=1, device_id={"lon": around(by), "lat": lat + 1}, device_id_type=MESH)

    for f, ref in enumerate((h_in, u_in, v_in)):
        state[f, :TOP, :] = jnp.zeros((TOP, lanes), jnp.float32)
        state[f, end:, :] = jnp.zeros((TOP, lanes), jnp.float32)
        middle[f, :8, :] = jnp.zeros((8, lanes), jnp.float32)
        middle[f, tall - 8 :, :] = jnp.zeros((8, lanes), jnp.float32)
        state[f, TOP:end, edge:] = jnp.zeros((rows, LANES), jnp.float32)
        state[f, TOP:end, :width] = ref[...]
    if plan.cols > 3 * part:
        work[:, 3 * part :, :] = jnp.zeros((2, plan.cols - 3 * part, lanes), jnp.bfloat16)

    blank = jnp.zeros((256 - rows, LANES), jnp.float32)
    for f in range(3):
        at = slice(HALO * f, HALO * f + HALO)
        first = jnp.concatenate([state[f, TOP:end, :LANES], blank], axis=0).T
        final = jnp.concatenate([state[f, TOP:end, edge:], blank], axis=0).T
        strips[0, at, :] = first[:HALO]
        strips[1, at, :] = final[off - HALO : off]
        lines[0, at, :] = state[f, TOP : TOP + HALO, :]
        lines[1, at, :] = state[f, end - HALO : end, :]
    strips[:, 12:, :] = jnp.zeros((2, 4, 256), jnp.float32)
    lines[:, 12:, :] = jnp.zeros((2, 4, lanes), jnp.float32)
    north_strips[...] = strips[...]

    @pl.when(lat == 0)
    def _():
        lane = lax.broadcasted_iota(jnp.int32, (16, 256), 1)
        row = lax.broadcasted_iota(jnp.int32, (16, 256), 0)
        flip = jnp.where(row < HALO, 1.0, -1.0)
        for side in range(2):
            strip = strips[side] * flip
            mirrored = jnp.zeros((16, 256), jnp.float32)
            for i in range(HALO):
                mirrored = jnp.where(lane == rows - 1 - i, strip[:, i : i + 1], mirrored)
            north_strips[side] = mirrored
        for f in range(3):
            sign = 1.0 if f == 0 else -1.0
            for i in range(HALO):
                lines[0, HALO * f + HALO - 1 - i, :] = sign * state[f, TOP + i, :]

    @pl.when(lat == last)
    def _():
        got_strips[:, 2] = jnp.zeros((2, 16, 256), jnp.float32)
        got_lines[1] = jnp.zeros((16, lanes), jnp.float32)

    inner = jnp.logical_and(lat > 0, lat < last)
    pl.semaphore_wait(barrier, jnp.where(inner, lons + 5, lons + 2))

    def strip_copy(source, side, slot, to_lon, to_lat, number):
        return pltpu.make_async_remote_copy(
            src_ref=source.at[side], dst_ref=got_strips.at[1 - side, slot],
            send_sem=strip_send.at[number, side], recv_sem=strip_recv.at[1 - side, slot],
            device_id={"lon": to_lon, "lat": to_lat}, device_id_type=MESH,
        )

    def line_copy(which, slot, to_lon, to_lat):
        return pltpu.make_async_remote_copy(
            src_ref=lines.at[which], dst_ref=got_lines.at[slot],
            send_sem=line_send.at[which], recv_sem=line_recv.at[slot],
            device_id={"lon": to_lon, "lat": to_lat}, device_id_type=MESH,
        )

    at_pole = lat == 0
    turn = jnp.where(at_pole, half, 0)
    to_north = jnp.where(at_pole, 0, lat - 1)
    north_line = line_copy(0, jnp.where(at_pole, 0, 1), around(turn), to_north)
    south_line = line_copy(1, 0, lon, lat + 1)
    north_slot = jnp.where(at_pole, 0, 2)
    north = [
        strip_copy(north_strips, 0, north_slot, around(turn - 1), to_north, 0),
        strip_copy(north_strips, 1, north_slot, around(turn + 1), to_north, 0),
    ]
    level = [strip_copy(strips, 0, 1, around(-1), lat, 1), strip_copy(strips, 1, 1, around(1), lat, 1)]
    south = [strip_copy(strips, 0, 0, around(-1), lat + 1, 2), strip_copy(strips, 1, 0, around(1), lat + 1, 2)]
    north_line.start()

    @pl.when(lat < last)
    def _():
        south_line.start()
        for copy in south:
            copy.start()

    for copy in level + north:
        copy.start()

    for copy in level:
        copy.wait()
    for copy in [north_line] + north:
        copy.wait_send()
    for side in range(2):
        strip_copy(strips, 1 - side, 0, lon, lat, 2).wait_recv()
    line_copy(1, 0, lon, lat).wait_recv()

    @pl.when(lat < last)
    def _():
        south_line.wait_send()
        for copy in south:
            copy.wait_send()
        for side in range(2):
            strip_copy(strips, 1 - side, 2, lon, lat, 2).wait_recv()
        line_copy(1, 1, lon, lat).wait_recv()

    lane = lax.broadcasted_iota(jnp.int32, (16, 256), 1)
    sides = []
    for side in (1, 0):
        sides.append(
            jnp.where(
                lane < TOP,
                pltpu.roll(got_strips[side, 0], (TOP - rows) % 256, 1),
                jnp.where(lane < end, pltpu.roll(got_strips[side, 1], TOP, 1), pltpu.roll(got_strips[side, 2], end, 1)),
            )
        )
    sides.append(jnp.zeros((LANES - 32, 256), jnp.float32))
    halo = jnp.concatenate(sides, axis=0).T[:tall]
    lane = lax.broadcasted_iota(jnp.int32, (tall, LANES), 1)
    for f in range(3):
        state[f, TOP - HALO : TOP, :] = got_lines[0, HALO * f : HALO * f + HALO, :]
        state[f, end : end + HALO, :] = got_lines[1, HALO * f : HALO * f + HALO, :]
        east = pltpu.roll(halo, (off - HALO * f) % LANES, 1)
        west = pltpu.roll(halo, (LANES - HALO - 16 - HALO * f) % LANES, 1)
        state[f, :, edge:] = jnp.where(
            lane >= LANES - HALO,
            west,
            jnp.where((lane >= off) & (lane < off + HALO), east, state[f, :, edge:]),
        )

    def south_rim(ref):
        @pl.when(lat == last)
        def _():
            for f in range(3):
                ref[f, end : end + 1, :] = ref[f, end - 1 : end, :]

    south_rim(state)
    get_rows.wait()
    get_waves.wait()

    for step in range(STEPS):
        stage(plan, geo, state, state, middle, 0.5 * TIME_STEP)
        south_rim(middle)
        stage(plan, geo, middle, state, state, TIME_STEP)

        @pl.loop(0, part // 16)
        def _(tile):
            lane = lax.broadcasted_iota(jnp.int32, (16, lanes), 1)
            start = pl.multiple_of(tile * 16, 16)
            for f in range(3):
                value = jnp.where(lane < width, state[f, pl.ds(start + 8, 16), :], 0.0)
                high, low = split(value)
                work[0, pl.ds(f * part + start, 16), :] = high
                work[1, pl.ds(f * part + start, 16), :] = low

        def against(table, value):
            return lax.dot_general(table, value, (((1,), (1,)), ((), ())), preferred_element_type=jnp.float32)

        for begin in range(0, plan.cols, 256):
            size = min(256, plan.cols - begin)
            high = work[0, begin : begin + size, :]
            low = work[1, begin : begin + size, :]
            total = against(waves[0], high) + (against(waves[0], low) + against(waves[1], high))
            parts[step, :, :, begin : begin + size] = total.reshape(lons, plan.pad, size)

        def scatter(by):
            return pltpu.make_async_remote_copy(
                src_ref=parts.at[step, around(by)], dst_ref=got_parts.at[step, by],
                send_sem=scatter_send.at[step, by], recv_sem=scatter_recv.at[step, by],
                device_id={"lon": around(by), "lat": lat}, device_id_type=MESH,
            )

        def gather(by):
            return pltpu.make_async_remote_copy(
                src_ref=whole.at[step, lon], dst_ref=whole.at[step, lon],
                send_sem=gather_send.at[step, by], recv_sem=gather_recv.at[step, by],
                device_id={"lon": around(by), "lat": lat}, device_id_type=MESH,
            )

        def arriving(by):
            return pltpu.make_async_remote_copy(
                src_ref=whole.at[step, lon], dst_ref=whole.at[step, around(-by)],
                send_sem=gather_send.at[step, by], recv_sem=gather_recv.at[step, by],
                device_id={"lon": around(by), "lat": lat}, device_id_type=MESH,
            )

        for by in range(1, lons):
            scatter(by).start()

        count = plan.filtered
        first_row = lat * rows - 8
        window = pltpu.roll(cut_ref[...], lax.rem(lats * count - first_row, count), 1)[:, :part]
        place = lax.broadcasted_iota(jnp.int32, (1, part), 1)
        for i in range(8):
            window = jnp.where(at_pole & (place == 7 - i), cut_ref[0:1, i : i + 1], window)
        cut = jnp.concatenate([window] * 3 + [jnp.zeros((1, plan.cols - 3 * part), jnp.int32)], axis=1)
        index = lon * plan.share + lax.broadcasted_iota(jnp.int32, (plan.pad, plan.cols), 0)
        wave = jnp.where(index <= KMAX, index, index - KMAX)
        scale = jnp.where(index == 0, 1.0 / NLON, 2.0 / NLON)
        weight = jnp.where(wave <= cut, scale, 0.0)

        total = parts[step, lon]
        for by in range(1, lons):
            scatter(by).wait()
            total = total + got_parts[step, by]
        whole[step, lon] = total * weight
        for by in range(1, lons):
            gather(by).start()
        for by in range(1, lons):
            gather(by).wait_send()
            arriving(by).wait_recv()

        high, low = split(whole[step].reshape(plan.waves, plan.cols).T)
        coeffs[0] = high
        coeffs[1] = low
        limit = count - first_row

        @pl.loop(0, lanes // 256)
        def _(chunk):
            at = pl.ds(pl.multiple_of(chunk * 256, 256), 256)
            thigh = waves[0, :, at]
            tlow = waves[1, :, at]
            row = lax.broadcasted_iota(jnp.int32, (part, 256), 0)
            for f in range(3):
                chigh = coeffs[0, f * part : (f + 1) * part, :]
                clow = coeffs[1, f * part : (f + 1) * part, :]
                value = jnp.dot(chigh, thigh, preferred_element_type=jnp.float32) + (
                    jnp.dot(chigh, tlow, preferred_element_type=jnp.float32)
                    + jnp.dot(clow, thigh, preferred_element_type=jnp.float32)
                )
                state[f, 8 : 8 + part, at] = jnp.where(row < limit, value, state[f, 8 : 8 + part, at])

        if step < STEPS - 1:
            south_rim(state)

    for f, ref in enumerate((h_out, u_out, v_out)):
        ref[...] = state[f, TOP:end, :width]


def shards(plan, height, east_wind, north_wind, cutoffs):
    f32, bf16 = jnp.float32, jnp.bfloat16
    vmem = pl.BlockSpec(memory_space=pltpu.VMEM)
    hbm = pl.BlockSpec(memory_space=pl.ANY)
    lons, tall, lanes = plan.lons, plan.tall, plan.lanes
    dma = pltpu.SemaphoreType.DMA
    block = (STEPS, lons, plan.pad, plan.cols)
    return pl.pallas_call(
        functools.partial(kernel, plan),
        out_shape=[jax.ShapeDtypeStruct(height.shape, f32)] * 3,
        in_specs=[vmem] * 4 + [hbm] * 2,
        out_specs=[vmem] * 3,
        scratch_shapes=[
            pltpu.VMEM((3, tall, lanes), f32),
            pltpu.VMEM((3, tall, lanes), f32),
            pltpu.VMEM((2, 16, 256), f32),
            pltpu.VMEM((2, 16, 256), f32),
            pltpu.VMEM((2, 3, 16, 256), f32),
            pltpu.VMEM((2, 16, lanes), f32),
            pltpu.VMEM((2, 16, lanes), f32),
            pltpu.VMEM((2, plan.waves, lanes), bf16),
            pltpu.VMEM((5, tall, LANES), f32),
            pltpu.VMEM((2, plan.cols, lanes), bf16),
            pltpu.VMEM(block, f32),
            pltpu.VMEM(block, f32),
            pltpu.VMEM(block, f32),
            pltpu.VMEM((2, plan.cols, plan.waves), bf16),
            dma((2,)),
            dma((3, 2)),
            dma((2, 3)),
            dma((2,)),
            dma((2,)),
            dma((STEPS, lons)),
            dma((STEPS, lons)),
            dma((STEPS, lons)),
            dma((STEPS, lons)),
        ],
        compiler_params=pltpu.CompilerParams(
            collective_id=0, has_side_effects=True, vmem_limit_bytes=48 * 1024 * 1024
        ),
    )(
        height, east_wind, north_wind, cutoffs.reshape(1, -1),
        jnp.asarray(wave_tables(plan)), jnp.asarray(row_tables(plan)),
    )


def solution(mesh):
    placed = (P("lat", "lon"), P("lat", "lon"), P("lat", "lon"), P())

    def program(height, east_wind, north_wind, cutoffs):
        lons, lats = mesh.shape["lon"], mesh.shape["lat"]
        rows, width = height.shape[0] // lats, height.shape[1] // lons
        plan = Plan(lons, lats, rows, width, cutoffs.shape[0])
        return jax.shard_map(
            lambda *blocks: tuple(shards(plan, *blocks)),
            mesh=mesh,
            in_specs=placed,
            out_specs=(P("lat", "lon"), P("lat", "lon"), P("lat", "lon")),
            check_vma=False,
        )(height, east_wind, north_wind, cutoffs)

    return program
```

```python
import functools
import math

import jax
import jax.numpy as jnp
import numpy as np
from jax import lax
from jax.experimental import pallas as pl
from jax.experimental.pallas import tpu as pltpu
from jax.sharding import PartitionSpec as P

NLON = 7200
LAT_ROWS = 3600
KMAX = 64
STEPS = 2
COURANT = 0.1
OMEGA_RATE = 1.5

LAT_STEP = math.pi / LAT_ROWS
LON_STEP = 2.0 * math.pi / NLON
TIME_STEP = COURANT * LAT_STEP
COEFFS = 2 * KMAX + 1
TOP = 16
HALO = 4
LANES = 128
MESH = pl.DeviceIdType.MESH


def up_to(value, multiple):
    return -(-value // multiple) * multiple


class Plan:
    def __init__(self, lons, lats, rows, width, filtered):
        self.lons, self.lats, self.rows, self.width = lons, lats, rows, width
        self.filtered = filtered
        self.lanes = up_to(width + 2 * HALO, LANES)
        self.tall = rows + 2 * TOP
        self.part = rows + TOP
        self.spread = self.lanes // LANES
        one = min(80, self.part - 16)
        two = self.part - one
        wide = up_to(3 * one, LANES)
        self.batches = ((8, one, 0, wide), (8 + one, two, wide, up_to(3 * two, LANES)))
        self.cols = wide + up_to(3 * two, LANES)
        self.share = up_to(COEFFS, lons) // lons
        self.pad = up_to(self.share, 8)
        self.waves = lons * self.pad


def wave_tables(plan):
    index = np.arange(plan.lons)[:, None] * plan.share + np.arange(plan.pad)[None, :]
    real = (np.arange(plan.pad)[None, :] < plan.share) & (index < COEFFS)
    index = np.where(real, index, 0).reshape(-1)
    wave = np.where(index <= KMAX, index, index - KMAX)
    lane = np.arange(plan.lanes)
    local = np.where(lane < plan.lanes - HALO, lane, lane - plan.lanes)
    column = np.arange(plan.lons)[:, None] * plan.width + local[None, :]
    turn = (wave[None, :, None] * column[:, None, :]) % NLON * (2.0 * math.pi / NLON)
    table = np.where((index <= KMAX)[None, :, None], np.cos(turn), np.sin(turn))
    table = np.where(real.reshape(-1)[None, :, None], table, 0.0).astype(np.float32)
    high = table.astype(jnp.bfloat16)
    low = (table - high.astype(np.float32)).astype(jnp.bfloat16)
    return np.stack([high, low], axis=1)


def row_tables(plan):
    row = np.arange(plan.lats)[:, None] * plan.rows + np.arange(plan.tall)[None, :] - TOP
    angle = (row + 0.5) * LAT_STEP
    cos = np.abs(np.sin(angle))
    north = np.abs(np.sin(angle - LAT_STEP))
    south = np.abs(np.sin(angle + LAT_STEP))
    signed = np.where(row < 0, -1.0, 1.0) / cos
    sin = np.cos(angle)
    half = 0.5 / LAT_STEP
    out = np.stack(
        [0.5 / LON_STEP * signed, half * north / cos, half * south / cos, 2.0 * OMEGA_RATE * sin, sin * signed],
        axis=1,
    )
    return np.broadcast_to(out[..., None], out.shape + (LANES,)).astype(np.float32)


def stage(plan, geo, source, base, target, factor, first, stop, work=None, at=0, rows=0):
    half = 0.5 / LAT_STEP
    spread = plan.spread
    off = plan.width - (plan.lanes - LANES)

    def piece(start, size, put):
        here = pl.ds(start, size)
        lane = lax.broadcasted_iota(jnp.int32, (size, LANES), 1)
        a, gn, gs, m3, q = (geo[g, here, :] for g in range(5))
        east, west, own = [], [], []
        for f in range(3):
            tiles = [source[f, c, here, :] for c in range(spread)]
            right = [pltpu.roll(tile, 1, 1) for tile in tiles]
            left = [pltpu.roll(tile, LANES - 1, 1) for tile in tiles]
            own.append(tiles)
            west.append([jnp.where(lane == 0, right[c - 1], right[c]) for c in range(spread)])
            east.append([jnp.where(lane == LANES - 1, left[(c + 1) % spread], left[c]) for c in range(spread)])
        for c in range(spread):
            h, u, v = (own[f][c] for f in range(3))
            hw, uw, vw = (west[f][c] for f in range(3))
            he, ue, ve = (east[f][c] for f in range(3))
            hn, un, vn = (source[f, c, pl.ds(start - 1, size), :] for f in range(3))
            hs, us, vs = (source[f, c, pl.ds(start + 1, size), :] for f in range(3))
            ua = u * a
            vb = v * half
            m = m3 + u * q
            fh = (hw * uw - he * ue) * a + (hs * vs * gs - hn * vn * gn)
            fu = m * v - ua * (ue - uw) - vb * (un - us) - (he - hw) * a
            fv = -(m * u) - ua * (ve - vw) - vb * (vn - vs) - half * (hn - hs)
            for f, rate in enumerate((fh, fu, fv)):
                value = base[f, c, here, :] + factor * rate
                target[f, c, here, :] = value
                if work is not None:
                    if c == spread - 1:
                        value = jnp.where(lane < off, value, 0.0)
                    high, low = split(value)
                    to = pl.ds(pl.multiple_of(at + f * rows + put, 16), size)
                    work[0, to, c * LANES : (c + 1) * LANES] = high
                    work[1, to, c * LANES : (c + 1) * LANES] = low

    pairs = (stop - first) // 2

    @pl.loop(0, pairs)
    def _(pair):
        piece(pl.multiple_of(pair * 16 + first * 8, 8), 16, pair * 16)

    if (stop - first) % 2:
        piece(stop * 8 - 8, 8, 0)


def split(value):
    high = value.astype(jnp.bfloat16)
    return high, (value - high.astype(jnp.float32)).astype(jnp.bfloat16)


def kernel(
    plan, h_in, u_in, v_in, cut_ref, waves_hbm, rows_hbm, h_out, u_out, v_out,
    state, middle, strips, north_strips, got_strips, lines, got_lines,
    waves, geo, work, parts, got_parts, whole, coeffs, weights,
    blocks, local_sem, strip_send, strip_recv, line_send, line_recv,
    scatter_send, scatter_recv, gather_send, gather_recv,
):
    lon = lax.axis_index("lon")
    lat = lax.axis_index("lat")
    lons, lats, rows, width, lanes = plan.lons, plan.lats, plan.rows, plan.width, plan.lanes
    tall, part, half = plan.tall, plan.part, plan.lons // 2
    last = lats - 1
    end = TOP + rows
    edge = lanes - LANES
    off = width - edge

    get_waves = pltpu.make_async_copy(waves_hbm.at[lon], waves, local_sem.at[0])
    get_rows = pltpu.make_async_copy(rows_hbm.at[lat], geo, local_sem.at[1])
    get_blocks = [
        pltpu.make_async_copy(ref, blocks.at[f], local_sem.at[2 + f]) for f, ref in enumerate((h_in, u_in, v_in))
    ]
    for copy in get_blocks:
        copy.start()
    get_rows.start()
    get_waves.start()

    def around(by):
        return lax.rem(lon + by + lons, lons)

    barrier = pltpu.get_barrier_semaphore()
    for by in range(1, lons):
        pl.semaphore_signal(barrier, inc=1, device_id={"lon": around(by), "lat": lat}, device_id_type=MESH)

    @pl.when(lat > 0)
    def _():
        for by in (-1, 0, 1):
            pl.semaphore_signal(barrier, inc=1, device_id={"lon": around(by), "lat": lat - 1}, device_id_type=MESH)

    @pl.when(lat < last)
    def _():
        for by in (-1, 0, 1):
            pl.semaphore_signal(barrier, inc=1, device_id={"lon": around(by), "lat": lat + 1}, device_id_type=MESH)

    spread = plan.spread
    rim = jnp.zeros((spread, TOP, LANES), jnp.float32)
    for f in range(3):
        state[f, :, :TOP, :] = rim
        state[f, :, end:, :] = rim
        middle[f, :, :8, :] = rim[:, :8]
        middle[f, :, tall - 8 :, :] = rim[:, :8]
        state[f, spread - 1, TOP:end, :] = jnp.zeros((rows, LANES), jnp.float32)
        get_blocks[f].wait()
        for c in range(spread):
            size = min(LANES, width - c * LANES)
            state[f, c, TOP:end, :size] = blocks[f, :, c * LANES : c * LANES + size]
    for _, count, begin, size in plan.batches:
        if size > 3 * count:
            work[:, begin + 3 * count : begin + size, :] = jnp.zeros((2, size - 3 * count, lanes), jnp.bfloat16)

    blank = jnp.zeros((256 - rows, LANES), jnp.float32)
    for f in range(3):
        at = slice(HALO * f, HALO * f + HALO)
        first = jnp.concatenate([state[f, 0, TOP:end, :], blank], axis=0).T
        final = jnp.concatenate([state[f, spread - 1, TOP:end, :], blank], axis=0).T
        strips[0, at, :] = first[:HALO]
        strips[1, at, :] = final[off - HALO : off]
        for c in range(spread):
            cut = slice(c * LANES, (c + 1) * LANES)
            lines[0, at, cut] = state[f, c, TOP : TOP + HALO, :]
            lines[1, at, cut] = state[f, c, end - HALO : end, :]
    strips[:, 12:, :] = jnp.zeros((2, 4, 256), jnp.float32)
    lines[:, 12:, :] = jnp.zeros((2, 4, lanes), jnp.float32)
    north_strips[...] = strips[...]

    @pl.when(lat == 0)
    def _():
        lane = lax.broadcasted_iota(jnp.int32, (16, 256), 1)
        row = lax.broadcasted_iota(jnp.int32, (16, 256), 0)
        flip = jnp.where(row < HALO, 1.0, -1.0)
        for side in range(2):
            strip = strips[side] * flip
            mirrored = jnp.zeros((16, 256), jnp.float32)
            for i in range(HALO):
                mirrored = jnp.where(lane == rows - 1 - i, strip[:, i : i + 1], mirrored)
            north_strips[side] = mirrored
        for f in range(3):
            sign = 1.0 if f == 0 else -1.0
            for i in range(HALO):
                for c in range(spread):
                    cut = slice(c * LANES, (c + 1) * LANES)
                    lines[0, HALO * f + HALO - 1 - i, cut] = sign * state[f, c, TOP + i, :]

    @pl.when(lat == last)
    def _():
        got_strips[:, 2] = jnp.zeros((2, 16, 256), jnp.float32)
        got_lines[1] = jnp.zeros((16, lanes), jnp.float32)

    inner = jnp.logical_and(lat > 0, lat < last)
    pl.semaphore_wait(barrier, jnp.where(inner, lons + 5, lons + 2))

    def strip_copy(source, side, slot, to_lon, to_lat, number):
        return pltpu.make_async_remote_copy(
            src_ref=source.at[side], dst_ref=got_strips.at[1 - side, slot],
            send_sem=strip_send.at[number, side], recv_sem=strip_recv.at[1 - side, slot],
            device_id={"lon": to_lon, "lat": to_lat}, device_id_type=MESH,
        )

    def line_copy(which, slot, to_lon, to_lat):
        return pltpu.make_async_remote_copy(
            src_ref=lines.at[which], dst_ref=got_lines.at[slot],
            send_sem=line_send.at[which], recv_sem=line_recv.at[slot],
            device_id={"lon": to_lon, "lat": to_lat}, device_id_type=MESH,
        )

    at_pole = lat == 0
    turn = jnp.where(at_pole, half, 0)
    to_north = jnp.where(at_pole, 0, lat - 1)
    north_line = line_copy(0, jnp.where(at_pole, 0, 1), around(turn), to_north)
    south_line = line_copy(1, 0, lon, lat + 1)
    north_slot = jnp.where(at_pole, 0, 2)
    north = [
        strip_copy(north_strips, 0, north_slot, around(turn - 1), to_north, 0),
        strip_copy(north_strips, 1, north_slot, around(turn + 1), to_north, 0),
    ]
    level = [strip_copy(strips, 0, 1, around(-1), lat, 1), strip_copy(strips, 1, 1, around(1), lat, 1)]
    south = [strip_copy(strips, 0, 0, around(-1), lat + 1, 2), strip_copy(strips, 1, 0, around(1), lat + 1, 2)]
    north_line.start()

    @pl.when(lat < last)
    def _():
        south_line.start()
        for copy in south:
            copy.start()

    for copy in level + north:
        copy.start()

    for copy in level:
        copy.wait()
    for copy in [north_line] + north:
        copy.wait_send()
    for side in range(2):
        strip_copy(strips, 1 - side, 0, lon, lat, 2).wait_recv()
    line_copy(1, 0, lon, lat).wait_recv()

    @pl.when(lat < last)
    def _():
        south_line.wait_send()
        for copy in south:
            copy.wait_send()
        for side in range(2):
            strip_copy(strips, 1 - side, 2, lon, lat, 2).wait_recv()
        line_copy(1, 1, lon, lat).wait_recv()

    lane = lax.broadcasted_iota(jnp.int32, (16, 256), 1)
    sides = []
    for side in (1, 0):
        sides.append(
            jnp.where(
                lane < TOP,
                pltpu.roll(got_strips[side, 0], (TOP - rows) % 256, 1),
                jnp.where(lane < end, pltpu.roll(got_strips[side, 1], TOP, 1), pltpu.roll(got_strips[side, 2], end, 1)),
            )
        )
    sides.append(jnp.zeros((LANES - 32, 256), jnp.float32))
    halo = jnp.concatenate(sides, axis=0).T[:tall]
    lane = lax.broadcasted_iota(jnp.int32, (tall, LANES), 1)
    for f in range(3):
        for c in range(spread):
            cut = slice(c * LANES, (c + 1) * LANES)
            state[f, c, TOP - HALO : TOP, :] = got_lines[0, HALO * f : HALO * f + HALO, cut]
            state[f, c, end : end + HALO, :] = got_lines[1, HALO * f : HALO * f + HALO, cut]
        east = pltpu.roll(halo, (off - HALO * f) % LANES, 1)
        west = pltpu.roll(halo, (LANES - HALO - 16 - HALO * f) % LANES, 1)
        state[f, spread - 1] = jnp.where(
            lane >= LANES - HALO,
            west,
            jnp.where((lane >= off) & (lane < off + HALO), east, state[f, spread - 1]),
        )

    def south_rim(ref):
        @pl.when(lat == last)
        def _():
            for f in range(3):
                ref[f, :, end : end + 1, :] = ref[f, :, end - 1 : end, :]

    south_rim(state)

    count = plan.filtered
    first_row = lat * rows - 8
    limit = count - first_row
    window = pltpu.roll(cut_ref[...], lax.rem(lats * count - first_row, count), 1)[:, : plan.part]
    place = lax.broadcasted_iota(jnp.int32, (1, plan.part), 1)
    for i in range(8):
        window = jnp.where(at_pole & (place == 7 - i), cut_ref[0:1, i : i + 1], window)
    index = lon * plan.share + lax.broadcasted_iota(jnp.int32, (plan.pad, 1), 0)
    wave = jnp.where(index <= KMAX, index, index - KMAX)
    scale = jnp.where(index == 0, 1.0 / NLON, 2.0 / NLON)
    for first, count, begin, size in plan.batches:
        cut = [window[:, first - 8 : first - 8 + count]] * 3
        if size > 3 * count:
            cut.append(jnp.zeros((1, size - 3 * count), jnp.int32))
        weights[:, begin : begin + size] = jnp.where(wave <= jnp.concatenate(cut, axis=1), scale, 0.0)

    get_rows.wait()
    get_waves.wait()
    table = waves[...].reshape(2 * plan.waves, lanes)

    def advance(first, stop):
        stage(plan, geo, state, state, middle, 0.5 * TIME_STEP, first, stop)

    def share_of(ref, step, place, batch):
        _, _, begin, size = plan.batches[batch]
        return ref.at[step, place, :, begin : begin + size]

    def scatter(step, batch, by):
        return pltpu.make_async_remote_copy(
            src_ref=share_of(parts, step, around(by), batch), dst_ref=share_of(got_parts, step, by, batch),
            send_sem=scatter_send.at[step, batch, by], recv_sem=scatter_recv.at[step, batch, by],
            device_id={"lon": around(by), "lat": lat}, device_id_type=MESH,
        )

    def gather(step, batch, by, place):
        return pltpu.make_async_remote_copy(
            src_ref=share_of(whole, step, lon, batch), dst_ref=share_of(whole, step, place, batch),
            send_sem=gather_send.at[step, batch, by], recv_sem=gather_recv.at[step, batch, by],
            device_id={"lon": around(by), "lat": lat}, device_id_type=MESH,
        )

    def project(step, batch):
        first, count, begin, size = plan.batches[batch]
        stage(
            plan, geo, middle, state, state, TIME_STEP, first // 8, (first + count) // 8, work, begin, count
        )

        def against(left, value):
            return lax.dot_general(left, value, (((1,), (1,)), ((), ())), preferred_element_type=jnp.float32)

        for left in range(begin, begin + size, 256):
            width = min(256, begin + size - left)
            both = against(table, work[0, left : left + width, :])
            total = both[: plan.waves] + (both[plan.waves :] + against(waves[0], work[1, left : left + width, :]))
            parts[step, :, :, left : left + width] = total.reshape(lons, plan.pad, width)[:, : plan.share]
        for by in range(1, lons):
            scatter(step, batch, by).start()

    def reduce(step, batch):
        _, _, begin, size = plan.batches[batch]
        at = pl.ds(begin, size)
        total = parts[step, lon, :, at]
        for by in range(1, lons):
            scatter(step, batch, by).wait()
            total = total + got_parts[step, by, :, at]
        whole[step, lon, :, at] = total * weights[0 : plan.share, at]
        for by in range(1, lons):
            gather(step, batch, by, lon).start()

    def expand(step, batch):
        first, count, begin, size = plan.batches[batch]
        for by in range(1, lons):
            gather(step, batch, by, lon).wait_send()
            gather(step, batch, by, around(-by)).wait_recv()
        got = whole[step, :, :, begin : begin + size]
        if plan.pad > plan.share:
            got = jnp.concatenate([got, jnp.zeros((lons, plan.pad - plan.share, size), jnp.float32)], axis=1)
        high, low = split(got.reshape(plan.waves, size).T)
        coeffs[0:size] = high
        coeffs[size : 2 * size] = low

        @pl.loop(0, spread // 2)
        def _(chunk):
            at = pl.ds(pl.multiple_of(chunk * 256, 256), 256)
            both = jnp.dot(coeffs[0 : 2 * size], waves[0, :, at], preferred_element_type=jnp.float32)
            value = both[:size] + (
                both[size:] + jnp.dot(coeffs[0:size], waves[1, :, at], preferred_element_type=jnp.float32)
            )
            row = lax.broadcasted_iota(jnp.int32, (count, LANES), 0) + (first - 8)
            for f in range(3):
                for c in range(2):
                    to = (f, chunk * 2 + c, pl.ds(first, count))
                    new = value[f * count : (f + 1) * count, c * LANES : (c + 1) * LANES]
                    state[to] = jnp.where(row < limit, new, state[to])

    tiles = tall // 8 - 1
    seam = plan.batches[1][0] // 8
    advance(1, seam + 1)
    for step in range(STEPS):
        project(step, 0)
        advance(seam + 1, tiles)
        south_rim(middle)
        project(step, 1)
        reduce(step, 0)
        reduce(step, 1)
        expand(step, 0)
        if step < STEPS - 1:
            advance(1, seam - 1)
            expand(step, 1)
            south_rim(state)
            advance(seam - 1, seam + 1)
        else:
            expand(step, 1)

    for f, ref in enumerate((h_out, u_out, v_out)):
        for c in range(spread):
            size = min(LANES, width - c * LANES)
            ref[:, c * LANES : c * LANES + size] = state[f, c, TOP:end, :size]


def shards(plan, height, east_wind, north_wind, cutoffs):
    f32, bf16 = jnp.float32, jnp.bfloat16
    vmem = pl.BlockSpec(memory_space=pltpu.VMEM)
    hbm = pl.BlockSpec(memory_space=pl.ANY)
    lons, tall, lanes = plan.lons, plan.tall, plan.lanes
    dma = pltpu.SemaphoreType.DMA
    block = (STEPS, lons, plan.share, plan.cols)
    return pl.pallas_call(
        functools.partial(kernel, plan),
        out_shape=[jax.ShapeDtypeStruct(height.shape, f32)] * 3,
        in_specs=[hbm] * 3 + [vmem] + [hbm] * 2,
        out_specs=[vmem] * 3,
        scratch_shapes=[
            pltpu.VMEM((3, plan.spread, tall, LANES), f32),
            pltpu.VMEM((3, plan.spread, tall, LANES), f32),
            pltpu.VMEM((2, 16, 256), f32),
            pltpu.VMEM((2, 16, 256), f32),
            pltpu.VMEM((2, 3, 16, 256), f32),
            pltpu.VMEM((2, 16, lanes), f32),
            pltpu.VMEM((2, 16, lanes), f32),
            pltpu.VMEM((2, plan.waves, lanes), bf16),
            pltpu.VMEM((5, tall, LANES), f32),
            pltpu.VMEM((2, plan.cols, lanes), bf16),
            pltpu.VMEM(block, f32),
            pltpu.VMEM(block, f32),
            pltpu.VMEM(block, f32),
            pltpu.VMEM((2 * max(batch[3] for batch in plan.batches), plan.waves), bf16),
            pltpu.VMEM((plan.pad, plan.cols), f32),
            pltpu.VMEM((3,) + height.shape, f32),
            dma((5,)),
            dma((3, 2)),
            dma((2, 3)),
            dma((2,)),
            dma((2,)),
            dma((STEPS, 2, lons)),
            dma((STEPS, 2, lons)),
            dma((STEPS, 2, lons)),
            dma((STEPS, 2, lons)),
        ],
        compiler_params=pltpu.CompilerParams(
            collective_id=0, has_side_effects=True, vmem_limit_bytes=60 * 1024 * 1024
        ),
    )(
        height, east_wind, north_wind, cutoffs.reshape(1, -1),
        jnp.asarray(wave_tables(plan)), jnp.asarray(row_tables(plan)),
    )


def solution(mesh):
    placed = (P("lat", "lon"), P("lat", "lon"), P("lat", "lon"), P())

    def program(height, east_wind, north_wind, cutoffs):
        lons, lats = mesh.shape["lon"], mesh.shape["lat"]
        rows, width = height.shape[0] // lats, height.shape[1] // lons
        plan = Plan(lons, lats, rows, width, cutoffs.shape[0])
        return jax.shard_map(
            lambda *blocks: tuple(shards(plan, *blocks)),
            mesh=mesh,
            in_specs=placed,
            out_specs=(P("lat", "lon"), P("lat", "lon"), P("lat", "lon")),
            check_vma=False,
        )(height, east_wind, north_wind, cutoffs)

    return program
```

```python
import functools
import math

import jax
import jax.numpy as jnp
import numpy as np
from jax import lax
from jax.experimental import pallas as pl
from jax.experimental.pallas import tpu as pltpu
from jax.sharding import PartitionSpec as P

NLON = 7200
LAT_ROWS = 3600
KMAX = 64
STEPS = 2
COURANT = 0.1
OMEGA_RATE = 1.5

LAT_STEP = math.pi / LAT_ROWS
LON_STEP = 2.0 * math.pi / NLON
TIME_STEP = COURANT * LAT_STEP
COEFFS = 2 * KMAX + 1
TOP = 16
HALO = 4
LANES = 128
MESH = pl.DeviceIdType.MESH


def up_to(value, multiple):
    return -(-value // multiple) * multiple


class Plan:
    def __init__(self, lons, lats, rows, width, filtered):
        self.lons, self.lats, self.rows, self.width = lons, lats, rows, width
        self.filtered = filtered
        self.lanes = up_to(width + 2 * HALO, LANES)
        self.tall = rows + 2 * TOP
        self.part = rows + TOP
        self.spread = self.lanes // LANES
        one = min(80, self.part - 16)
        two = self.part - one
        wide = up_to(3 * one, LANES)
        self.batches = ((8, one, 0, wide), (8 + one, two, wide, up_to(3 * two, LANES)))
        self.cols = wide + up_to(3 * two, LANES)
        self.share = up_to(COEFFS, lons) // lons
        self.pad = up_to(self.share, 8)
        self.waves = lons * self.pad


def wave_tables(plan):
    index = np.arange(plan.lons)[:, None] * plan.share + np.arange(plan.pad)[None, :]
    real = (np.arange(plan.pad)[None, :] < plan.share) & (index < COEFFS)
    index = np.where(real, index, 0).reshape(-1)
    wave = np.where(index <= KMAX, index, index - KMAX)
    lane = np.arange(plan.lanes)
    local = np.where(lane < plan.lanes - HALO, lane, lane - plan.lanes)
    column = np.arange(plan.lons)[:, None] * plan.width + local[None, :]
    turn = (wave[None, :, None] * column[:, None, :]) % NLON * (2.0 * math.pi / NLON)
    table = np.where((index <= KMAX)[None, :, None], np.cos(turn), np.sin(turn))
    table = np.where(real.reshape(-1)[None, :, None], table, 0.0).astype(np.float32)
    high = table.astype(jnp.bfloat16)
    low = (table - high.astype(np.float32)).astype(jnp.bfloat16)
    return np.stack([high, low], axis=1)


def row_tables(plan):
    row = np.arange(plan.lats)[:, None] * plan.rows + np.arange(plan.tall)[None, :] - TOP
    angle = (row + 0.5) * LAT_STEP
    cos = np.abs(np.sin(angle))
    north = np.abs(np.sin(angle - LAT_STEP))
    south = np.abs(np.sin(angle + LAT_STEP))
    signed = np.where(row < 0, -1.0, 1.0) / cos
    sin = np.cos(angle)
    half = 0.5 / LAT_STEP
    out = np.stack(
        [0.5 / LON_STEP * signed, half * north / cos, half * south / cos, 2.0 * OMEGA_RATE * sin, sin * signed],
        axis=1,
    )
    return np.broadcast_to(out[..., None], out.shape + (LANES,)).astype(np.float32)


def stage(plan, geo, source, base, target, factor, first, stop, work=None, at=0, rows=0, cs=None):
    half = 0.5 / LAT_STEP
    spread = plan.spread
    off = plan.width - (plan.lanes - LANES)
    cs = range(spread) if cs is None else cs

    def piece(start, size, put):
        here = pl.ds(start, size)
        lane = lax.broadcasted_iota(jnp.int32, (size, LANES), 1)
        a, gn, gs, m3, q = (geo[g, here, :] for g in range(5))
        kept = {}

        def rolled(f, c, by):
            c = c % spread
            if (f, c, by) not in kept:
                kept[f, c, by] = pltpu.roll(source[f, c, here, :], by, 1)
            return kept[f, c, by]

        def west(f, c):
            return jnp.where(lane == 0, rolled(f, c - 1, 1), rolled(f, c, 1))

        def east(f, c):
            return jnp.where(lane == LANES - 1, rolled(f, c + 1, LANES - 1), rolled(f, c, LANES - 1))

        for c in cs:
            h, u, v = (source[f, c, here, :] for f in range(3))
            hw, uw, vw = (west(f, c) for f in range(3))
            he, ue, ve = (east(f, c) for f in range(3))
            hn, un, vn = (source[f, c, pl.ds(start - 1, size), :] for f in range(3))
            hs, us, vs = (source[f, c, pl.ds(start + 1, size), :] for f in range(3))
            ua = u * a
            vb = v * half
            m = m3 + u * q
            fh = (hw * uw - he * ue) * a + (hs * vs * gs - hn * vn * gn)
            fu = m * v - ua * (ue - uw) - vb * (un - us) - (he - hw) * a
            fv = -(m * u) - ua * (ve - vw) - vb * (vn - vs) - half * (hn - hs)
            for f, rate in enumerate((fh, fu, fv)):
                value = base[f, c, here, :] + factor * rate
                target[f, c, here, :] = value
                if work is not None:
                    if c == spread - 1:
                        value = jnp.where(lane < off, value, 0.0)
                    high, low = split(value)
                    to = pl.ds(pl.multiple_of(at + f * rows + put, 16), size)
                    work[0, to, c * LANES : (c + 1) * LANES] = high
                    work[1, to, c * LANES : (c + 1) * LANES] = low

    pairs = (stop - first) // 2

    @pl.loop(0, pairs)
    def _(pair):
        piece(pl.multiple_of(pair * 16 + first * 8, 8), 16, pair * 16)

    if (stop - first) % 2:
        piece(stop * 8 - 8, 8, 0)


def split(value):
    high = value.astype(jnp.bfloat16)
    return high, (value - high.astype(jnp.float32)).astype(jnp.bfloat16)


def kernel(
    plan, h_in, u_in, v_in, cut_ref, waves_hbm, rows_hbm, h_out, u_out, v_out,
    state, middle, strips, north_strips, got_strips, lines, got_lines,
    waves, geo, work, parts, got_parts, whole, coeffs, weights,
    blocks, local_sem, strip_send, strip_recv, line_send, line_recv,
    scatter_send, scatter_recv, gather_send, gather_recv,
):
    lon = lax.axis_index("lon")
    lat = lax.axis_index("lat")
    lons, lats, rows, width, lanes = plan.lons, plan.lats, plan.rows, plan.width, plan.lanes
    tall, part, half = plan.tall, plan.part, plan.lons // 2
    last = lats - 1
    end = TOP + rows
    edge = lanes - LANES
    off = width - edge

    get_waves = pltpu.make_async_copy(waves_hbm.at[lon], waves, local_sem.at[0])
    get_rows = pltpu.make_async_copy(rows_hbm.at[lat], geo, local_sem.at[1])
    get_blocks = [
        pltpu.make_async_copy(ref, blocks.at[f], local_sem.at[2 + f]) for f, ref in enumerate((h_in, u_in, v_in))
    ]
    for copy in get_blocks:
        copy.start()
    get_rows.start()
    get_waves.start()

    def around(by):
        return lax.rem(lon + by + lons, lons)

    barrier = pltpu.get_barrier_semaphore()
    for by in range(1, lons):
        pl.semaphore_signal(barrier, inc=1, device_id={"lon": around(by), "lat": lat}, device_id_type=MESH)

    @pl.when(lat > 0)
    def _():
        for by in (-1, 0, 1):
            pl.semaphore_signal(barrier, inc=1, device_id={"lon": around(by), "lat": lat - 1}, device_id_type=MESH)

    @pl.when(lat < last)
    def _():
        for by in (-1, 0, 1):
            pl.semaphore_signal(barrier, inc=1, device_id={"lon": around(by), "lat": lat + 1}, device_id_type=MESH)

    spread = plan.spread
    rim = jnp.zeros((spread, TOP, LANES), jnp.float32)
    for f in range(3):
        state[f, :, :TOP, :] = rim
        state[f, :, end:, :] = rim
        middle[f, :, :8, :] = rim[:, :8]
        middle[f, :, tall - 8 :, :] = rim[:, :8]
        state[f, spread - 1, TOP:end, :] = jnp.zeros((rows, LANES), jnp.float32)
        get_blocks[f].wait()
        for c in range(spread):
            size = min(LANES, width - c * LANES)
            state[f, c, TOP:end, :size] = blocks[f, :, c * LANES : c * LANES + size]
    for _, count, begin, size in plan.batches:
        if size > 3 * count:
            work[:, begin + 3 * count : begin + size, :] = jnp.zeros((2, size - 3 * count, lanes), jnp.bfloat16)

    blank = jnp.zeros((256 - rows, LANES), jnp.float32)
    for f in range(3):
        at = slice(HALO * f, HALO * f + HALO)
        first = jnp.concatenate([state[f, 0, TOP:end, :], blank], axis=0).T
        final = jnp.concatenate([state[f, spread - 1, TOP:end, :], blank], axis=0).T
        strips[0, at, :] = first[:HALO]
        strips[1, at, :] = final[off - HALO : off]
        for c in range(spread):
            cut = slice(c * LANES, (c + 1) * LANES)
            lines[0, at, cut] = state[f, c, TOP : TOP + HALO, :]
            lines[1, at, cut] = state[f, c, end - HALO : end, :]
    strips[:, 12:, :] = jnp.zeros((2, 4, 256), jnp.float32)
    lines[:, 12:, :] = jnp.zeros((2, 4, lanes), jnp.float32)
    north_strips[...] = strips[...]

    @pl.when(lat == 0)
    def _():
        lane = lax.broadcasted_iota(jnp.int32, (16, 256), 1)
        row = lax.broadcasted_iota(jnp.int32, (16, 256), 0)
        flip = jnp.where(row < HALO, 1.0, -1.0)
        for side in range(2):
            strip = strips[side] * flip
            mirrored = jnp.zeros((16, 256), jnp.float32)
            for i in range(HALO):
                mirrored = jnp.where(lane == rows - 1 - i, strip[:, i : i + 1], mirrored)
            north_strips[side] = mirrored
        for f in range(3):
            sign = 1.0 if f == 0 else -1.0
            for i in range(HALO):
                for c in range(spread):
                    cut = slice(c * LANES, (c + 1) * LANES)
                    lines[0, HALO * f + HALO - 1 - i, cut] = sign * state[f, c, TOP + i, :]

    @pl.when(lat == last)
    def _():
        got_strips[:, 2] = jnp.zeros((2, 16, 256), jnp.float32)
        got_lines[1] = jnp.zeros((16, lanes), jnp.float32)

    inner = jnp.logical_and(lat > 0, lat < last)
    pl.semaphore_wait(barrier, jnp.where(inner, lons + 5, lons + 2))

    def strip_copy(source, side, slot, to_lon, to_lat, number):
        return pltpu.make_async_remote_copy(
            src_ref=source.at[side], dst_ref=got_strips.at[1 - side, slot],
            send_sem=strip_send.at[number, side], recv_sem=strip_recv.at[1 - side, slot],
            device_id={"lon": to_lon, "lat": to_lat}, device_id_type=MESH,
        )

    def line_copy(which, slot, to_lon, to_lat):
        return pltpu.make_async_remote_copy(
            src_ref=lines.at[which], dst_ref=got_lines.at[slot],
            send_sem=line_send.at[which], recv_sem=line_recv.at[slot],
            device_id={"lon": to_lon, "lat": to_lat}, device_id_type=MESH,
        )

    at_pole = lat == 0
    turn = jnp.where(at_pole, half, 0)
    to_north = jnp.where(at_pole, 0, lat - 1)
    north_line = line_copy(0, jnp.where(at_pole, 0, 1), around(turn), to_north)
    south_line = line_copy(1, 0, lon, lat + 1)
    north_slot = jnp.where(at_pole, 0, 2)
    north = [
        strip_copy(north_strips, 0, north_slot, around(turn - 1), to_north, 0),
        strip_copy(north_strips, 1, north_slot, around(turn + 1), to_north, 0),
    ]
    level = [strip_copy(strips, 0, 1, around(-1), lat, 1), strip_copy(strips, 1, 1, around(1), lat, 1)]
    south = [strip_copy(strips, 0, 0, around(-1), lat + 1, 2), strip_copy(strips, 1, 0, around(1), lat + 1, 2)]
    north_line.start()

    @pl.when(lat < last)
    def _():
        south_line.start()
        for copy in south:
            copy.start()

    for copy in level + north:
        copy.start()

    get_rows.wait()
    near, far = TOP // 8 + 1, end // 8 - 1
    inside = range(1, spread - 1)
    outside = (0, spread - 1)

    def advance(first, stop, cs=None):
        stage(plan, geo, state, state, middle, 0.5 * TIME_STEP, first, stop, cs=cs)

    advance(near, far, inside)

    for copy in level:
        copy.wait()
    for copy in [north_line] + north:
        copy.wait_send()
    for side in range(2):
        strip_copy(strips, 1 - side, 0, lon, lat, 2).wait_recv()
    line_copy(1, 0, lon, lat).wait_recv()

    @pl.when(lat < last)
    def _():
        south_line.wait_send()
        for copy in south:
            copy.wait_send()
        for side in range(2):
            strip_copy(strips, 1 - side, 2, lon, lat, 2).wait_recv()
        line_copy(1, 1, lon, lat).wait_recv()

    lane = lax.broadcasted_iota(jnp.int32, (16, 256), 1)
    sides = []
    for side in (1, 0):
        sides.append(
            jnp.where(
                lane < TOP,
                pltpu.roll(got_strips[side, 0], (TOP - rows) % 256, 1),
                jnp.where(lane < end, pltpu.roll(got_strips[side, 1], TOP, 1), pltpu.roll(got_strips[side, 2], end, 1)),
            )
        )
    sides.append(jnp.zeros((LANES - 32, 256), jnp.float32))
    halo = jnp.concatenate(sides, axis=0).T[:tall]
    lane = lax.broadcasted_iota(jnp.int32, (tall, LANES), 1)
    for f in range(3):
        for c in range(spread):
            cut = slice(c * LANES, (c + 1) * LANES)
            state[f, c, TOP - HALO : TOP, :] = got_lines[0, HALO * f : HALO * f + HALO, cut]
            state[f, c, end : end + HALO, :] = got_lines[1, HALO * f : HALO * f + HALO, cut]
        east = pltpu.roll(halo, (off - HALO * f) % LANES, 1)
        west = pltpu.roll(halo, (LANES - HALO - 16 - HALO * f) % LANES, 1)
        state[f, spread - 1] = jnp.where(
            lane >= LANES - HALO,
            west,
            jnp.where((lane >= off) & (lane < off + HALO), east, state[f, spread - 1]),
        )

    def south_rim(ref):
        @pl.when(lat == last)
        def _():
            for f in range(3):
                ref[f, :, end : end + 1, :] = ref[f, :, end - 1 : end, :]

    south_rim(state)

    count = plan.filtered
    first_row = lat * rows - 8
    limit = count - first_row
    window = pltpu.roll(cut_ref[...], lax.rem(lats * count - first_row, count), 1)[:, : plan.part]
    place = lax.broadcasted_iota(jnp.int32, (1, plan.part), 1)
    for i in range(8):
        window = jnp.where(at_pole & (place == 7 - i), cut_ref[0:1, i : i + 1], window)
    index = lon * plan.share + lax.broadcasted_iota(jnp.int32, (plan.pad, 1), 0)
    wave = jnp.where(index <= KMAX, index, index - KMAX)
    scale = jnp.where(index == 0, 1.0 / NLON, 2.0 / NLON)
    for first, count, begin, size in plan.batches:
        cut = [window[:, first - 8 : first - 8 + count]] * 3
        if size > 3 * count:
            cut.append(jnp.zeros((1, size - 3 * count), jnp.int32))
        weights[:, begin : begin + size] = jnp.where(wave <= jnp.concatenate(cut, axis=1), scale, 0.0)

    get_waves.wait()
    table = waves[...].reshape(2 * plan.waves, lanes)

    def share_of(ref, step, place, batch):
        _, _, begin, size = plan.batches[batch]
        return ref.at[step, place, :, begin : begin + size]

    def scatter(step, batch, by):
        return pltpu.make_async_remote_copy(
            src_ref=share_of(parts, step, around(by), batch), dst_ref=share_of(got_parts, step, by, batch),
            send_sem=scatter_send.at[step, batch, by], recv_sem=scatter_recv.at[step, batch, by],
            device_id={"lon": around(by), "lat": lat}, device_id_type=MESH,
        )

    def gather(step, batch, by, place):
        return pltpu.make_async_remote_copy(
            src_ref=share_of(whole, step, lon, batch), dst_ref=share_of(whole, step, place, batch),
            send_sem=gather_send.at[step, batch, by], recv_sem=gather_recv.at[step, batch, by],
            device_id={"lon": around(by), "lat": lat}, device_id_type=MESH,
        )

    def finish(batch):
        first, count, begin, size = plan.batches[batch]
        stage(
            plan, geo, middle, state, state, TIME_STEP, first // 8, (first + count) // 8, work, begin, count
        )

    def project(step, batch):
        _, _, begin, size = plan.batches[batch]

        def against(left, value):
            return lax.dot_general(left, value, (((1,), (1,)), ((), ())), preferred_element_type=jnp.float32)

        for left in range(begin, begin + size, 256):
            width = min(256, begin + size - left)
            both = against(table, work[0, left : left + width, :])
            total = both[: plan.waves] + (both[plan.waves :] + against(waves[0], work[1, left : left + width, :]))
            parts[step, :, :, left : left + width] = total.reshape(lons, plan.pad, width)[:, : plan.share]
        for by in range(1, lons):
            scatter(step, batch, by).start()

    def reduce(step, batch):
        _, _, begin, size = plan.batches[batch]
        at = pl.ds(begin, size)
        total = parts[step, lon, :, at]
        for by in range(1, lons):
            scatter(step, batch, by).wait()
            total = total + got_parts[step, by, :, at]
        whole[step, lon, :, at] = total * weights[0 : plan.share, at]
        for by in range(1, lons):
            gather(step, batch, by, lon).start()

    def expand(step, batch):
        first, count, begin, size = plan.batches[batch]
        for by in range(1, lons):
            gather(step, batch, by, lon).wait_send()
            gather(step, batch, by, around(-by)).wait_recv()
        got = whole[step, :, :, begin : begin + size]
        if plan.pad > plan.share:
            got = jnp.concatenate([got, jnp.zeros((lons, plan.pad - plan.share, size), jnp.float32)], axis=1)
        high, low = split(got.reshape(plan.waves, size).T)
        coeffs[0:size] = high
        coeffs[size : 2 * size] = low

        @pl.loop(0, spread // 2)
        def _(chunk):
            at = pl.ds(pl.multiple_of(chunk * 256, 256), 256)
            both = jnp.dot(coeffs[0 : 2 * size], waves[0, :, at], preferred_element_type=jnp.float32)
            value = both[:size] + (
                both[size:] + jnp.dot(coeffs[0:size], waves[1, :, at], preferred_element_type=jnp.float32)
            )
            row = lax.broadcasted_iota(jnp.int32, (count, LANES), 0) + (first - 8)
            for f in range(3):
                for c in range(2):
                    to = (f, chunk * 2 + c, pl.ds(first, count))
                    new = value[f * count : (f + 1) * count, c * LANES : (c + 1) * LANES]
                    state[to] = jnp.where(row < limit, new, state[to])

    tiles = tall // 8 - 1
    seam = plan.batches[1][0] // 8
    outs = (h_out, u_out, v_out)

    def given(f, begin, stop):
        span = pl.ds(begin, stop - begin)
        number = 5 + f + (3 if begin else 0)
        return pltpu.make_async_copy(blocks.at[f, span], outs[f].at[span], local_sem.at[number])

    def give(begin, stop):
        for f in range(3):
            for c in range(spread):
                size = min(LANES, width - c * LANES)
                blocks[f, begin:stop, c * LANES : c * LANES + size] = state[f, c, TOP + begin : TOP + stop, :size]
            given(f, begin, stop).start()

    advance(1, near)
    advance(near, seam + 1, outside)
    for step in range(STEPS):
        finish(0)
        project(step, 0)
        if step == 0:
            advance(seam + 1, far, outside)
            advance(far, tiles)
        else:
            advance(seam + 1, tiles)
        south_rim(middle)
        finish(1)
        reduce(step, 0)
        project(step, 1)
        expand(step, 0)
        reduce(step, 1)
        if step < STEPS - 1:
            advance(1, seam - 1)
            expand(step, 1)
            south_rim(state)
            advance(seam - 1, seam + 1)
        else:
            split_row = seam * 8 - TOP
            give(0, split_row)
            expand(step, 1)
            give(split_row, rows)
            for f in range(3):
                given(f, 0, split_row).wait()
                given(f, split_row, rows).wait()


def hand_over(rows, *refs):
    sources, targets, sem = refs[:3], refs[3:6], refs[6]
    half = up_to(rows // 2, 8)
    copies = []
    for f in range(3):
        for i, span in enumerate((pl.ds(0, half), pl.ds(half, rows - half))):
            copies.append(pltpu.make_async_copy(sources[f].at[span], targets[f].at[span], sem.at[2 * f + i]))
    for copy in copies:
        copy.start()
    for copy in copies:
        copy.wait()


def shards(plan, height, east_wind, north_wind, cutoffs):
    f32, bf16 = jnp.float32, jnp.bfloat16
    vmem = pl.BlockSpec(memory_space=pltpu.VMEM)
    hbm = pl.BlockSpec(memory_space=pltpu.HBM)
    lons, tall, lanes = plan.lons, plan.tall, plan.lanes
    dma = pltpu.SemaphoreType.DMA
    block = (STEPS, lons, plan.share, plan.cols)
    shapes = [jax.ShapeDtypeStruct(height.shape, f32)] * 3
    params = pltpu.CompilerParams(vmem_limit_bytes=60 * 1024 * 1024)
    final = pl.pallas_call(
        functools.partial(kernel, plan),
        out_shape=shapes,
        in_specs=[hbm] * 3 + [vmem] + [hbm] * 2,
        out_specs=[hbm] * 3,
        scratch_shapes=[
            pltpu.VMEM((3, plan.spread, tall, LANES), f32),
            pltpu.VMEM((3, plan.spread, tall, LANES), f32),
            pltpu.VMEM((2, 16, 256), f32),
            pltpu.VMEM((2, 16, 256), f32),
            pltpu.VMEM((2, 3, 16, 256), f32),
            pltpu.VMEM((2, 16, lanes), f32),
            pltpu.VMEM((2, 16, lanes), f32),
            pltpu.VMEM((2, plan.waves, lanes), bf16),
            pltpu.VMEM((5, tall, LANES), f32),
            pltpu.VMEM((2, plan.cols, lanes), bf16),
            pltpu.VMEM(block, f32),
            pltpu.VMEM(block, f32),
            pltpu.VMEM(block, f32),
            pltpu.VMEM((2 * max(batch[3] for batch in plan.batches), plan.waves), bf16),
            pltpu.VMEM((plan.pad, plan.cols), f32),
            pltpu.VMEM((3,) + height.shape, f32),
            dma((11,)),
            dma((3, 2)),
            dma((2, 3)),
            dma((2,)),
            dma((2,)),
            dma((STEPS, 2, lons)),
            dma((STEPS, 2, lons)),
            dma((STEPS, 2, lons)),
            dma((STEPS, 2, lons)),
        ],
        compiler_params=pltpu.CompilerParams(
            collective_id=0, has_side_effects=True, vmem_limit_bytes=60 * 1024 * 1024
        ),
    )(
        height, east_wind, north_wind, cutoffs.reshape(1, -1),
        jnp.asarray(wave_tables(plan)), jnp.asarray(row_tables(plan)),
    )
    return pl.pallas_call(
        functools.partial(hand_over, height.shape[0]),
        out_shape=shapes,
        in_specs=[hbm] * 3,
        out_specs=[hbm] * 3,
        scratch_shapes=[dma((6,))],
        compiler_params=params,
    )(*final)


def solution(mesh):
    placed = (P("lat", "lon"), P("lat", "lon"), P("lat", "lon"), P())

    def program(height, east_wind, north_wind, cutoffs):
        lons, lats = mesh.shape["lon"], mesh.shape["lat"]
        rows, width = height.shape[0] // lats, height.shape[1] // lons
        plan = Plan(lons, lats, rows, width, cutoffs.shape[0])
        return jax.shard_map(
            lambda *blocks: tuple(shards(plan, *blocks)),
            mesh=mesh,
            in_specs=placed,
            out_specs=(P("lat", "lon"), P("lat", "lon"), P("lat", "lon")),
            check_vma=False,
        )(height, east_wind, north_wind, cutoffs)

    return program
```

```python
import functools
import math

import jax
import jax.numpy as jnp
import numpy as np
from jax import lax
from jax.experimental import pallas as pl
from jax.experimental.pallas import tpu as pltpu
from jax.sharding import PartitionSpec as P

NLON = 7200
LAT_ROWS = 3600
KMAX = 64
STEPS = 2
COURANT = 0.1
OMEGA_RATE = 1.5

LAT_STEP = math.pi / LAT_ROWS
LON_STEP = 2.0 * math.pi / NLON
TIME_STEP = COURANT * LAT_STEP
COEFFS = 2 * KMAX + 1
TOP = 16
HALO = 4
LANES = 128
MESH = pl.DeviceIdType.MESH


def up_to(value, multiple):
    return -(-value // multiple) * multiple


class Plan:
    def __init__(self, lons, lats, rows, width, filtered):
        self.lons, self.lats, self.rows, self.width = lons, lats, rows, width
        self.filtered = filtered
        self.lanes = up_to(width + 2 * HALO, LANES)
        self.tall = rows + 2 * TOP
        self.part = rows + TOP
        self.spread = self.lanes // LANES
        one = min(80, self.part - 16)
        two = self.part - one
        wide = up_to(3 * one, LANES)
        self.batches = ((8, one, 0, wide), (8 + one, two, wide, up_to(3 * two, LANES)))
        self.cols = wide + up_to(3 * two, LANES)
        self.share = up_to(COEFFS, lons) // lons
        self.pad = up_to(self.share, 8)
        self.waves = lons * self.pad


def wave_tables(plan):
    index = np.arange(plan.lons)[:, None] * plan.share + np.arange(plan.pad)[None, :]
    real = (np.arange(plan.pad)[None, :] < plan.share) & (index < COEFFS)
    index = np.where(real, index, 0).reshape(-1)
    wave = np.where(index <= KMAX, index, index - KMAX)
    lane = np.arange(plan.lanes)
    local = np.where(lane < plan.lanes - HALO, lane, lane - plan.lanes)
    column = np.arange(plan.lons)[:, None] * plan.width + local[None, :]
    turn = (wave[None, :, None] * column[:, None, :]) % NLON * (2.0 * math.pi / NLON)
    table = np.where((index <= KMAX)[None, :, None], np.cos(turn), np.sin(turn))
    table = np.where(real.reshape(-1)[None, :, None], table, 0.0).astype(np.float32)
    high = table.astype(jnp.bfloat16)
    low = (table - high.astype(np.float32)).astype(jnp.bfloat16)
    return np.stack([high, low], axis=1)


def row_tables(plan):
    row = np.arange(plan.lats)[:, None] * plan.rows + np.arange(plan.tall)[None, :] - TOP
    angle = (row + 0.5) * LAT_STEP
    cos = np.abs(np.sin(angle))
    north = np.abs(np.sin(angle - LAT_STEP))
    south = np.abs(np.sin(angle + LAT_STEP))
    signed = np.where(row < 0, -1.0, 1.0) / cos
    sin = np.cos(angle)
    half = 0.5 / LAT_STEP
    out = np.stack(
        [0.5 / LON_STEP * signed, half * north / cos, half * south / cos, 2.0 * OMEGA_RATE * sin, sin * signed],
        axis=1,
    )
    return np.broadcast_to(out[..., None], out.shape + (LANES,)).astype(np.float32)


def stage(plan, geo, source, base, target, factor, first, stop, work=None, at=0, rows=0):
    half = 0.5 / LAT_STEP
    spread = plan.spread
    off = plan.width - (plan.lanes - LANES)

    def piece(start, size, put):
        here = pl.ds(start, size)
        lane = lax.broadcasted_iota(jnp.int32, (size, LANES), 1)
        a, gn, gs, m3, q = (geo[g, here, :] for g in range(5))
        east, west, own = [], [], []
        for f in range(3):
            tiles = [source[f, c, here, :] for c in range(spread)]
            right = [pltpu.roll(tile, 1, 1) for tile in tiles]
            left = [pltpu.roll(tile, LANES - 1, 1) for tile in tiles]
            own.append(tiles)
            west.append([jnp.where(lane == 0, right[c - 1], right[c]) for c in range(spread)])
            east.append([jnp.where(lane == LANES - 1, left[(c + 1) % spread], left[c]) for c in range(spread)])
        for c in range(spread):
            h, u, v = (own[f][c] for f in range(3))
            hw, uw, vw = (west[f][c] for f in range(3))
            he, ue, ve = (east[f][c] for f in range(3))
            hn, un, vn = (source[f, c, pl.ds(start - 1, size), :] for f in range(3))
            hs, us, vs = (source[f, c, pl.ds(start + 1, size), :] for f in range(3))
            ua = u * a
            vb = v * half
            m = m3 + u * q
            fh = (hw * uw - he * ue) * a + (hs * vs * gs - hn * vn * gn)
            fu = m * v - ua * (ue - uw) - vb * (un - us) - (he - hw) * a
            fv = -(m * u) - ua * (ve - vw) - vb * (vn - vs) - half * (hn - hs)
            for f, rate in enumerate((fh, fu, fv)):
                value = base[f, c, here, :] + factor * rate
                target[f, c, here, :] = value
                if work is not None:
                    if c == spread - 1:
                        value = jnp.where(lane < off, value, 0.0)
                    high, low = split(value)
                    to = pl.ds(pl.multiple_of(at + f * rows + put, 16), size)
                    work[0, to, c * LANES : (c + 1) * LANES] = high
                    work[1, to, c * LANES : (c + 1) * LANES] = low

    pairs = (stop - first) // 2

    @pl.loop(0, pairs)
    def _(pair):
        piece(pl.multiple_of(pair * 16 + first * 8, 8), 16, pair * 16)

    if (stop - first) % 2:
        piece(stop * 8 - 8, 8, 0)


def split(value):
    high = value.astype(jnp.bfloat16)
    return high, (value - high.astype(jnp.float32)).astype(jnp.bfloat16)


def kernel(
    plan, h_in, u_in, v_in, cut_ref, waves_hbm, rows_hbm, h_out, u_out, v_out,
    state, middle, strips, north_strips, got_strips, lines, got_lines,
    waves, geo, work, parts, got_parts, whole, coeffs, weights,
    blocks, local_sem, strip_send, strip_recv, line_send, line_recv,
    scatter_send, scatter_recv, gather_send, gather_recv,
):
    lon = lax.axis_index("lon")
    lat = lax.axis_index("lat")
    lons, lats, rows, width, lanes = plan.lons, plan.lats, plan.rows, plan.width, plan.lanes
    tall, part, half = plan.tall, plan.part, plan.lons // 2
    last = lats - 1
    end = TOP + rows
    edge = lanes - LANES
    off = width - edge

    get_waves = pltpu.make_async_copy(waves_hbm.at[lon], waves, local_sem.at[0])
    get_rows = pltpu.make_async_copy(rows_hbm.at[lat], geo, local_sem.at[1])
    get_blocks = [
        pltpu.make_async_copy(ref, blocks.at[f], local_sem.at[2 + f]) for f, ref in enumerate((h_in, u_in, v_in))
    ]
    for copy in get_blocks:
        copy.start()
    get_rows.start()
    get_waves.start()

    def around(by):
        return lax.rem(lon + by + lons, lons)

    barrier = pltpu.get_barrier_semaphore()
    for by in range(1, lons):
        pl.semaphore_signal(barrier, inc=1, device_id={"lon": around(by), "lat": lat}, device_id_type=MESH)

    @pl.when(lat > 0)
    def _():
        for by in (-1, 0, 1):
            pl.semaphore_signal(barrier, inc=1, device_id={"lon": around(by), "lat": lat - 1}, device_id_type=MESH)

    @pl.when(lat < last)
    def _():
        for by in (-1, 0, 1):
            pl.semaphore_signal(barrier, inc=1, device_id={"lon": around(by), "lat": lat + 1}, device_id_type=MESH)

    spread = plan.spread
    rim = jnp.zeros((spread, TOP, LANES), jnp.float32)
    for f in range(3):
        state[f, :, :TOP, :] = rim
        state[f, :, end:, :] = rim
        middle[f, :, :8, :] = rim[:, :8]
        middle[f, :, tall - 8 :, :] = rim[:, :8]
        state[f, spread - 1, TOP:end, :] = jnp.zeros((rows, LANES), jnp.float32)
        get_blocks[f].wait()
        for c in range(spread):
            size = min(LANES, width - c * LANES)
            state[f, c, TOP:end, :size] = blocks[f, :, c * LANES : c * LANES + size]
    for _, count, begin, size in plan.batches:
        if size > 3 * count:
            work[:, begin + 3 * count : begin + size, :] = jnp.zeros((2, size - 3 * count, lanes), jnp.bfloat16)

    blank = jnp.zeros((256 - rows, LANES), jnp.float32)
    for f in range(3):
        at = slice(HALO * f, HALO * f + HALO)
        first = jnp.concatenate([state[f, 0, TOP:end, :], blank], axis=0).T
        final = jnp.concatenate([state[f, spread - 1, TOP:end, :], blank], axis=0).T
        strips[0, at, :] = first[:HALO]
        strips[1, at, :] = final[off - HALO : off]
        for c in range(spread):
            cut = slice(c * LANES, (c + 1) * LANES)
            lines[0, at, cut] = state[f, c, TOP : TOP + HALO, :]
            lines[1, at, cut] = state[f, c, end - HALO : end, :]
    strips[:, 12:, :] = jnp.zeros((2, 4, 256), jnp.float32)
    lines[:, 12:, :] = jnp.zeros((2, 4, lanes), jnp.float32)
    north_strips[...] = strips[...]

    @pl.when(lat == 0)
    def _():
        lane = lax.broadcasted_iota(jnp.int32, (16, 256), 1)
        row = lax.broadcasted_iota(jnp.int32, (16, 256), 0)
        flip = jnp.where(row < HALO, 1.0, -1.0)
        for side in range(2):
            strip = strips[side] * flip
            mirrored = jnp.zeros((16, 256), jnp.float32)
            for i in range(HALO):
                mirrored = jnp.where(lane == rows - 1 - i, strip[:, i : i + 1], mirrored)
            north_strips[side] = mirrored
        for f in range(3):
            sign = 1.0 if f == 0 else -1.0
            for i in range(HALO):
                for c in range(spread):
                    cut = slice(c * LANES, (c + 1) * LANES)
                    lines[0, HALO * f + HALO - 1 - i, cut] = sign * state[f, c, TOP + i, :]

    @pl.when(lat == last)
    def _():
        got_strips[:, 2] = jnp.zeros((2, 16, 256), jnp.float32)
        got_lines[1] = jnp.zeros((16, lanes), jnp.float32)

    inner = jnp.logical_and(lat > 0, lat < last)
    pl.semaphore_wait(barrier, jnp.where(inner, lons + 5, lons + 2))

    def strip_copy(source, side, slot, to_lon, to_lat, number):
        return pltpu.make_async_remote_copy(
            src_ref=source.at[side], dst_ref=got_strips.at[1 - side, slot],
            send_sem=strip_send.at[number, side], recv_sem=strip_recv.at[1 - side, slot],
            device_id={"lon": to_lon, "lat": to_lat}, device_id_type=MESH,
        )

    def line_copy(which, slot, to_lon, to_lat):
        return pltpu.make_async_remote_copy(
            src_ref=lines.at[which], dst_ref=got_lines.at[slot],
            send_sem=line_send.at[which], recv_sem=line_recv.at[slot],
            device_id={"lon": to_lon, "lat": to_lat}, device_id_type=MESH,
        )

    at_pole = lat == 0
    turn = jnp.where(at_pole, half, 0)
    to_north = jnp.where(at_pole, 0, lat - 1)
    north_line = line_copy(0, jnp.where(at_pole, 0, 1), around(turn), to_north)
    south_line = line_copy(1, 0, lon, lat + 1)
    north_slot = jnp.where(at_pole, 0, 2)
    north = [
        strip_copy(north_strips, 0, north_slot, around(turn - 1), to_north, 0),
        strip_copy(north_strips, 1, north_slot, around(turn + 1), to_north, 0),
    ]
    level = [strip_copy(strips, 0, 1, around(-1), lat, 1), strip_copy(strips, 1, 1, around(1), lat, 1)]
    south = [strip_copy(strips, 0, 0, around(-1), lat + 1, 2), strip_copy(strips, 1, 0, around(1), lat + 1, 2)]
    north_line.start()

    @pl.when(lat < last)
    def _():
        south_line.start()
        for copy in south:
            copy.start()

    for copy in level + north:
        copy.start()

    for copy in level:
        copy.wait()
    for copy in [north_line] + north:
        copy.wait_send()
    for side in range(2):
        strip_copy(strips, 1 - side, 0, lon, lat, 2).wait_recv()
    line_copy(1, 0, lon, lat).wait_recv()

    @pl.when(lat < last)
    def _():
        south_line.wait_send()
        for copy in south:
            copy.wait_send()
        for side in range(2):
            strip_copy(strips, 1 - side, 2, lon, lat, 2).wait_recv()
        line_copy(1, 1, lon, lat).wait_recv()

    lane = lax.broadcasted_iota(jnp.int32, (16, 256), 1)
    sides = []
    for side in (1, 0):
        sides.append(
            jnp.where(
                lane < TOP,
                pltpu.roll(got_strips[side, 0], (TOP - rows) % 256, 1),
                jnp.where(lane < end, pltpu.roll(got_strips[side, 1], TOP, 1), pltpu.roll(got_strips[side, 2], end, 1)),
            )
        )
    sides.append(jnp.zeros((LANES - 32, 256), jnp.float32))
    halo = jnp.concatenate(sides, axis=0).T[:tall]
    lane = lax.broadcasted_iota(jnp.int32, (tall, LANES), 1)
    for f in range(3):
        for c in range(spread):
            cut = slice(c * LANES, (c + 1) * LANES)
            state[f, c, TOP - HALO : TOP, :] = got_lines[0, HALO * f : HALO * f + HALO, cut]
            state[f, c, end : end + HALO, :] = got_lines[1, HALO * f : HALO * f + HALO, cut]
        east = pltpu.roll(halo, (off - HALO * f) % LANES, 1)
        west = pltpu.roll(halo, (LANES - HALO - 16 - HALO * f) % LANES, 1)
        state[f, spread - 1] = jnp.where(
            lane >= LANES - HALO,
            west,
            jnp.where((lane >= off) & (lane < off + HALO), east, state[f, spread - 1]),
        )

    def south_rim(ref):
        @pl.when(lat == last)
        def _():
            for f in range(3):
                ref[f, :, end : end + 1, :] = ref[f, :, end - 1 : end, :]

    south_rim(state)

    count = plan.filtered
    first_row = lat * rows - 8
    limit = count - first_row
    window = pltpu.roll(cut_ref[...], lax.rem(lats * count - first_row, count), 1)[:, : plan.part]
    place = lax.broadcasted_iota(jnp.int32, (1, plan.part), 1)
    for i in range(8):
        window = jnp.where(at_pole & (place == 7 - i), cut_ref[0:1, i : i + 1], window)
    index = lon * plan.share + lax.broadcasted_iota(jnp.int32, (plan.pad, 1), 0)
    wave = jnp.where(index <= KMAX, index, index - KMAX)
    scale = jnp.where(index == 0, 1.0 / NLON, 2.0 / NLON)
    for first, count, begin, size in plan.batches:
        cut = [window[:, first - 8 : first - 8 + count]] * 3
        if size > 3 * count:
            cut.append(jnp.zeros((1, size - 3 * count), jnp.int32))
        weights[:, begin : begin + size] = jnp.where(wave <= jnp.concatenate(cut, axis=1), scale, 0.0)

    get_rows.wait()
    get_waves.wait()
    table = waves[...].reshape(2 * plan.waves, lanes)

    def advance(first, stop):
        stage(plan, geo, state, state, middle, 0.5 * TIME_STEP, first, stop)

    def share_of(ref, step, place, batch):
        _, _, begin, size = plan.batches[batch]
        return ref.at[step, place, :, begin : begin + size]

    def scatter(step, batch, by):
        return pltpu.make_async_remote_copy(
            src_ref=share_of(parts, step, around(by), batch), dst_ref=share_of(got_parts, step, by, batch),
            send_sem=scatter_send.at[step, batch, by], recv_sem=scatter_recv.at[step, batch, by],
            device_id={"lon": around(by), "lat": lat}, device_id_type=MESH,
        )

    def gather(step, batch, by, place):
        return pltpu.make_async_remote_copy(
            src_ref=share_of(whole, step, lon, batch), dst_ref=share_of(whole, step, place, batch),
            send_sem=gather_send.at[step, batch, by], recv_sem=gather_recv.at[step, batch, by],
            device_id={"lon": around(by), "lat": lat}, device_id_type=MESH,
        )

    def project(step, batch):
        first, count, begin, size = plan.batches[batch]
        stage(
            plan, geo, middle, state, state, TIME_STEP, first // 8, (first + count) // 8, work, begin, count
        )

        def against(left, value):
            return lax.dot_general(left, value, (((1,), (1,)), ((), ())), preferred_element_type=jnp.float32)

        for left in range(begin, begin + size, 256):
            width = min(256, begin + size - left)
            both = against(table, work[0, left : left + width, :])
            total = both[: plan.waves] + (both[plan.waves :] + against(waves[0], work[1, left : left + width, :]))
            parts[step, :, :, left : left + width] = total.reshape(lons, plan.pad, width)[:, : plan.share]
        for by in range(1, lons):
            scatter(step, batch, by).start()

    def reduce(step, batch):
        _, _, begin, size = plan.batches[batch]
        at = pl.ds(begin, size)
        total = parts[step, lon, :, at]
        for by in range(1, lons):
            scatter(step, batch, by).wait()
            total = total + got_parts[step, by, :, at]
        whole[step, lon, :, at] = total * weights[0 : plan.share, at]
        for by in range(1, lons):
            gather(step, batch, by, lon).start()

    def expand(step, batch):
        first, count, begin, size = plan.batches[batch]
        for by in range(1, lons):
            gather(step, batch, by, lon).wait_send()
            gather(step, batch, by, around(-by)).wait_recv()
        got = whole[step, :, :, begin : begin + size]
        if plan.pad > plan.share:
            got = jnp.concatenate([got, jnp.zeros((lons, plan.pad - plan.share, size), jnp.float32)], axis=1)
        high, low = split(got.reshape(plan.waves, size).T)
        coeffs[0:size] = high
        coeffs[size : 2 * size] = low

        @pl.loop(0, spread // 2)
        def _(chunk):
            at = pl.ds(pl.multiple_of(chunk * 256, 256), 256)
            both = jnp.dot(coeffs[0 : 2 * size], waves[0, :, at], preferred_element_type=jnp.float32)
            value = both[:size] + (
                both[size:] + jnp.dot(coeffs[0:size], waves[1, :, at], preferred_element_type=jnp.float32)
            )
            row = lax.broadcasted_iota(jnp.int32, (count, LANES), 0) + (first - 8)
            for f in range(3):
                for c in range(2):
                    to = (f, chunk * 2 + c, pl.ds(first, count))
                    new = value[f * count : (f + 1) * count, c * LANES : (c + 1) * LANES]
                    state[to] = jnp.where(row < limit, new, state[to])

    tiles = tall // 8 - 1
    seam = plan.batches[1][0] // 8
    advance(1, seam + 1)
    for step in range(STEPS):
        project(step, 0)
        advance(seam + 1, tiles)
        south_rim(middle)
        project(step, 1)
        reduce(step, 0)
        reduce(step, 1)
        expand(step, 0)
        if step < STEPS - 1:
            advance(1, seam - 1)
            expand(step, 1)
            south_rim(state)
            advance(seam - 1, seam + 1)
        else:
            expand(step, 1)

    for f, ref in enumerate((h_out, u_out, v_out)):
        for c in range(spread):
            size = min(LANES, width - c * LANES)
            ref[:, c * LANES : c * LANES + size] = state[f, c, TOP:end, :size]


def hand_over(rows, *refs):
    sources, targets, held, sem = refs[:3], refs[3:6], refs[6], refs[7]
    half = up_to(rows // 2, 8)
    reads, writes = [], []
    for f in range(3):
        for i, span in enumerate((pl.ds(0, half), pl.ds(half, rows - half))):
            here = held.at[f, span]
            reads.append(pltpu.make_async_copy(sources[f].at[span], here, sem.at[0, 2 * f + i]))
            writes.append(pltpu.make_async_copy(here, targets[f].at[span], sem.at[1, 2 * f + i]))
    for copy in reads:
        copy.start()
    for read, write in zip(reads, writes):
        read.wait()
        write.start()
    for copy in writes:
        copy.wait()


def shards(plan, height, east_wind, north_wind, cutoffs):
    f32, bf16 = jnp.float32, jnp.bfloat16
    vmem = pl.BlockSpec(memory_space=pltpu.VMEM)
    hbm = pl.BlockSpec(memory_space=pl.ANY)
    lons, tall, lanes = plan.lons, plan.tall, plan.lanes
    dma = pltpu.SemaphoreType.DMA
    block = (STEPS, lons, plan.share, plan.cols)
    shapes = [jax.ShapeDtypeStruct(height.shape, f32)] * 3
    final = pl.pallas_call(
        functools.partial(kernel, plan),
        out_shape=shapes,
        in_specs=[hbm] * 3 + [vmem] + [hbm] * 2,
        out_specs=[vmem] * 3,
        scratch_shapes=[
            pltpu.VMEM((3, plan.spread, tall, LANES), f32),
            pltpu.VMEM((3, plan.spread, tall, LANES), f32),
            pltpu.VMEM((2, 16, 256), f32),
            pltpu.VMEM((2, 16, 256), f32),
            pltpu.VMEM((2, 3, 16, 256), f32),
            pltpu.VMEM((2, 16, lanes), f32),
            pltpu.VMEM((2, 16, lanes), f32),
            pltpu.VMEM((2, plan.waves, lanes), bf16),
            pltpu.VMEM((5, tall, LANES), f32),
            pltpu.VMEM((2, plan.cols, lanes), bf16),
            pltpu.VMEM(block, f32),
            pltpu.VMEM(block, f32),
            pltpu.VMEM(block, f32),
            pltpu.VMEM((2 * max(batch[3] for batch in plan.batches), plan.waves), bf16),
            pltpu.VMEM((plan.pad, plan.cols), f32),
            pltpu.VMEM((3,) + height.shape, f32),
            dma((5,)),
            dma((3, 2)),
            dma((2, 3)),
            dma((2,)),
            dma((2,)),
            dma((STEPS, 2, lons)),
            dma((STEPS, 2, lons)),
            dma((STEPS, 2, lons)),
            dma((STEPS, 2, lons)),
        ],
        compiler_params=pltpu.CompilerParams(
            collective_id=0, has_side_effects=True, vmem_limit_bytes=60 * 1024 * 1024
        ),
    )(
        height, east_wind, north_wind, cutoffs.reshape(1, -1),
        jnp.asarray(wave_tables(plan)), jnp.asarray(row_tables(plan)),
    )
    return pl.pallas_call(
        functools.partial(hand_over, height.shape[0]),
        out_shape=shapes,
        in_specs=[hbm] * 3,
        out_specs=[hbm] * 3,
        scratch_shapes=[pltpu.VMEM((3,) + height.shape, f32), dma((2, 6))],
        compiler_params=pltpu.CompilerParams(vmem_limit_bytes=60 * 1024 * 1024),
    )(*final)


def solution(mesh):
    placed = (P("lat", "lon"), P("lat", "lon"), P("lat", "lon"), P())

    def program(height, east_wind, north_wind, cutoffs):
        lons, lats = mesh.shape["lon"], mesh.shape["lat"]
        rows, width = height.shape[0] // lats, height.shape[1] // lons
        plan = Plan(lons, lats, rows, width, cutoffs.shape[0])
        return jax.shard_map(
            lambda *blocks: tuple(shards(plan, *blocks)),
            mesh=mesh,
            in_specs=placed,
            out_specs=(P("lat", "lon"), P("lat", "lon"), P("lat", "lon")),
            check_vma=False,
        )(height, east_wind, north_wind, cutoffs)

    return program
```
